32 devices in a mesh: row: 8 (over y, x, core), col: 4 (over z).
Axes of the slice: x: 2, y: 2, z: 4, core: 2. Of those that a mesh axis runs over, the one named last changes fastest.
Arguments:
- traces: bfloat16 [2048, 64, 512], P(('row', 'col')), may hold values from -6 to 6
- live_flags: int32 [2048], P(('row', 'col')), may hold values 0 or 1
Outputs:
- correlations: bfloat16 [2048, 2048, 128], P('row', 'col')
The draws below stay inside these ranges and needn't reach their ends.
Inputs may be any that keep to these rules, and one draw needn't show every extreme that they name: `live_flags`: 1 marks a working channel.
All inputs are finite; a program needn't handle non-finite values. No bound on the sum of `live_flags` on one device may be relied on, other than what follows from the above.
Results may differ from the reference program's by a relative error of at most 0.0058.
Values may be sent and summed in bfloat16 or wider, within the bound.
A program may use at most 448 MiB of HBM per device.

```python
import math
import jax
import jax.numpy as jnp
from jax import lax

C = 2048
F = 256
LAGS = 128
SAMP = 512
NW = 64
N_ROW = 8
N_COL = 4


def plant(array, own_key, low, high):
    shape = array.shape
    spot = [jax.random.randint(jax.random.fold_in(own_key, axis), (), 0, shape[axis]) for axis in range(len(shape))]
    array = array.at[tuple(spot)].set(low)
    longest = shape.index(max(shape))
    spot[longest] = (spot[longest] + 1) % shape[longest]
    return array.at[tuple(spot)].set(high)


def level_of(stream_key, dims, split, low, high):
    def one(position, shards_of):
        draws = jax.random.uniform(jax.random.fold_in(jax.random.fold_in(stream_key, 6), position), (shards_of,), jnp.float32, low / len(split), high / len(split))
        return jnp.repeat(jnp.exp(draws), dims[position] // shards_of).reshape((-1,) + (1,) * (len(dims) - position - 1))

    factor_of = one(*split[0])
    for cut in split[1:]:
        factor_of = factor_of * one(*cut)
    return factor_of


def gaussian(rng, dims, deviation, limit, split=(), kind=jnp.bfloat16):
    factor_of = level_of(rng, dims, split, -0.22, 0.18) if split else 1.0
    array = jax.random.normal(rng, dims, jnp.float32) * deviation * factor_of
    return jnp.minimum(jnp.maximum(array, -limit), limit).astype(kind)


def setup_inputs(seed: int = 0) -> dict:
    splits = jax.random.split(jax.random.key(seed), 3)
    traces = gaussian(splits[0], (C, NW, SAMP), 1.0, 6.0, ((0, 32),))
    live_flags = plant((jax.random.randint(splits[1], (C,), 0, 8) < 7).astype(jnp.int32), jax.random.fold_in(splits[1], 1), 0, 1)
    return dict(traces=traces, live_flags=live_flags)


def make_tables():
    samples = jnp.arange(SAMP, dtype=jnp.int32)
    bins = jnp.arange(F, dtype=jnp.int32)
    phase = samples[:, None] * bins[None, :] % SAMP
    angle = 2.0 * math.pi * phase.astype(jnp.float32) / SAMP
    forward = jnp.concatenate([jnp.cos(angle), -jnp.sin(angle)], axis=1)
    taper = 0.5 - 0.5 * jnp.cos(2.0 * math.pi * samples.astype(jnp.float32) / SAMP)
    near = (jnp.abs(bins[:, None] - bins[None, :]) <= 4).astype(jnp.float32)
    counts = lax.optimization_barrier(jnp.sum(near, axis=0))
    lagval = jnp.arange(LAGS, dtype=jnp.int32) - LAGS // 2
    lphase = bins[:, None] * lagval[None, :] % SAMP
    langle = 2.0 * math.pi * lphase.astype(jnp.float32) / SAMP
    inverse = jnp.concatenate([jnp.cos(langle), -jnp.sin(langle)], axis=0).astype(jnp.bfloat16)
    return (forward, taper, near, counts, inverse)

def whiten(traces, live_flags):
    forward, taper, near, counts, inverse = make_tables()
    chans = traces.shape[0]
    tapered = traces.astype(jnp.float32) * taper
    spectra = jnp.dot(tapered.reshape(-1, SAMP), forward, precision=lax.Precision.HIGHEST)
    real_part = spectra[:, :F]
    imag_part = spectra[:, F:]
    power = real_part * real_part + imag_part * imag_part
    smooth = jnp.dot(power, near, precision=lax.Precision.HIGHEST) / counts
    level = lax.optimization_barrier(jnp.mean(power, axis=1, keepdims=True))
    scale = 1.0 / jnp.sqrt(smooth + 0.05 * level + 1e-06)
    alive = jnp.repeat(live_flags.astype(jnp.float32), NW)[:, None]
    white = jnp.concatenate([real_part * scale, imag_part * scale], axis=1) * alive
    white = white.reshape(chans, NW, 2, F)
    white = jnp.transpose(white, (3, 0, 2, 1)).reshape(F, chans, 2 * NW)
    return white.astype(jnp.bfloat16)

def reference(traces, live_flags):
    forward, taper, near, counts, inverse = make_tables()
    white = whiten(traces, live_flags)
    per_dev = C // (N_ROW * N_COL)
    block = per_dev * N_ROW
    index = jnp.arange(C, dtype=jnp.int32)
    order = (index % block // per_dev * N_COL + index // block) * per_dev + index % per_dev
    second = white[:, order, :].astype(jnp.float32)
    rows = C // N_ROW
    firsts = jnp.transpose(white.reshape(F, N_ROW, rows, 2 * NW), (1, 0, 2, 3))

    def one_block(item):
        first, start = item
        first = first.astype(jnp.float32)
        turned = jnp.concatenate([first[..., NW:], -first[..., :NW]], axis=2)
        cross_re = jnp.einsum('fik,fjk->fij', first, second)
        cross_im = jnp.einsum('fik,fjk->fij', turned, second)
        stacked = (jnp.concatenate([cross_re, cross_im], axis=0) / math.sqrt(NW)).astype(jnp.bfloat16)
        corr = lax.dot_general(stacked, inverse, (((0,), (0,)), ((), ())), preferred_element_type=jnp.float32)
        corr = corr / math.sqrt(F)
        chan_i = start + jnp.arange(rows, dtype=jnp.int32)
        same = chan_i[:, None] == order[None, :]
        corr = jnp.where(same[:, :, None], 0.0, corr)
        return corr.astype(jnp.bfloat16)
    starts = jnp.arange(N_ROW, dtype=jnp.int32) * rows
    result = lax.map(one_block, (firsts, starts))
    return result.reshape(C, C, LAGS)
```

```python
import functools
import math

import jax
import jax.numpy as jnp
from jax import lax
from jax.experimental import pallas as pl
from jax.experimental.pallas import tpu as pltpu
from jax.sharding import PartitionSpec as P

F = 256
LAGS = 128
SAMP = 512
NW = 64


def make_tables():
    samples = jnp.arange(SAMP, dtype=jnp.int32)
    bins = jnp.arange(F, dtype=jnp.int32)
    phase = samples[:, None] * bins[None, :] % SAMP
    angle = 2.0 * math.pi * phase.astype(jnp.float32) / SAMP
    forward = jnp.concatenate([jnp.cos(angle), -jnp.sin(angle)], axis=1)
    taper = 0.5 - 0.5 * jnp.cos(2.0 * math.pi * samples.astype(jnp.float32) / SAMP)
    near = (jnp.abs(bins[:, None] - bins[None, :]) <= 4).astype(jnp.float32)
    counts = jnp.sum(near, axis=0)
    lagval = jnp.arange(LAGS, dtype=jnp.int32) - LAGS // 2
    lphase = bins[:, None] * lagval[None, :] % SAMP
    langle = 2.0 * math.pi * lphase.astype(jnp.float32) / SAMP
    inverse = jnp.concatenate([jnp.cos(langle), -jnp.sin(langle)], axis=0).astype(jnp.bfloat16)
    return (forward, taper, near, counts, inverse)


def whiten(traces, live_flags, forward, taper, near, counts):
    chans = traces.shape[0]
    tapered = traces.astype(jnp.float32) * taper
    spectra = jnp.dot(tapered.reshape(-1, SAMP), forward, precision=lax.Precision.HIGHEST)
    real_part = spectra[:, :F]
    imag_part = spectra[:, F:]
    power = real_part * real_part + imag_part * imag_part
    smooth = jnp.dot(power, near, precision=lax.Precision.HIGHEST) / counts
    level = jnp.mean(power, axis=1, keepdims=True)
    scale = 1.0 / jnp.sqrt(smooth + 0.05 * level + 1e-06)
    alive = jnp.repeat(live_flags.astype(jnp.float32), NW)[:, None]
    real_white = (real_part * scale * alive).astype(jnp.bfloat16)
    imag_white = (imag_part * scale * alive).astype(jnp.bfloat16)
    real_white = jnp.transpose(real_white.reshape(chans, NW, F), (2, 0, 1))
    imag_white = jnp.transpose(imag_white.reshape(chans, NW, F), (2, 0, 1))
    return jnp.concatenate([real_white, imag_white], axis=2)


def slab_kernel(n_parts, n_f, fb, ib, has_out, base_ref, *refs):
    parts = refs[:n_parts]
    second_ref, table_ref, chan_j_ref = refs[n_parts : n_parts + 3]
    out_ref, scratch = refs[-2:]
    step = pl.program_id(1)
    rows = sum(part.shape[1] for part in parts)

    @pl.when(step < n_f)
    def _():
        lane = lax.broadcasted_iota(jnp.int32, (rows, 2 * NW), 1)
        sign = jnp.where(lane < NW, 1.0, -1.0)
        for b in range(fb):
            pieces = [part[b] for part in parts]
            first = pieces[0] if n_parts == 1 else jnp.concatenate(pieces, axis=0)
            turned = (pltpu.roll(first.astype(jnp.float32), NW, 1) * sign).astype(jnp.bfloat16)
            both = jnp.concatenate([first, turned], axis=0)
            cross = lax.dot_general(
                both, second_ref[b], (((1,), (1,)), ((), ())), preferred_element_type=jnp.float32
            )
            at = step * fb + b
            for c in range(scratch.shape[0]):
                lanes = slice(c * 128, (c + 1) * 128)
                scratch[c, pl.ds(at, rows, stride=2 * F), :] = cross[:rows, lanes]
                scratch[c, pl.ds(at + F, rows, stride=2 * F), :] = cross[rows:, lanes]

    @pl.when(step >= n_f)
    def _():
        group = step - n_f
        chan_j = chan_j_ref[...]
        for r in range(ib):
            start = pl.multiple_of((group * ib + r) * (2 * F), 2 * F)
            for c in range(scratch.shape[0]):
                stacked = scratch[c, pl.ds(start, 2 * F), :].astype(jnp.bfloat16)
                corr = jnp.dot(table_ref[...], stacked, preferred_element_type=jnp.float32)
                chan_i = base_ref[base_ref.shape[0] - 1] + base_ref[group] * ib + r
                keep = jnp.where(chan_j[:, c * 128 : (c + 1) * 128] == chan_i, 0.0, SCALE)
                corr = jnp.transpose(corr * keep)
                out_ref[r, c * 128 : (c + 1) * 128, :] = corr.astype(jnp.bfloat16)


def slab(parts, second, table, chan_j, base, total_rows, out):
    rows = sum(part.shape[1] for part in parts)
    cols = second.shape[1]
    ib, fb = 8, 16
    jt = min(256, cols)
    n_f, n_i = F // fb, rows // ib
    f_of = lambda p: jnp.minimum(p, n_f - 1)
    in_specs = [
        pl.BlockSpec((fb, part.shape[1], 2 * NW), lambda j, p, s: (f_of(p), 0, 0))
        for part in parts
    ]
    in_specs += [
        pl.BlockSpec((fb, jt, 2 * NW), lambda j, p, s: (f_of(p), j, 0)),
        pl.BlockSpec((LAGS, 2 * F), lambda j, p, s: (0, 0)),
        pl.BlockSpec((1, jt), lambda j, p, s: (0, j)),
    ]
    args = [*parts, second, table, chan_j]
    aliases = {}
    if out is not None:
        in_specs.append(pl.BlockSpec(memory_space=pl.ANY))
        aliases = {1 + len(args): 0}
        args.append(out)
    return pl.pallas_call(
        functools.partial(slab_kernel, len(parts), n_f, fb, ib, out is not None),
        out_shape=jax.ShapeDtypeStruct((total_rows, cols, LAGS), jnp.bfloat16),
        grid_spec=pltpu.PrefetchScalarGridSpec(
            num_scalar_prefetch=1,
            grid=(cols // jt, n_f + n_i),
            in_specs=in_specs,
            out_specs=pl.BlockSpec(
                (ib, jt, LAGS), lambda j, p, s: (s[jnp.maximum(p - n_f, 0)], j, 0)
            ),
            scratch_shapes=[pltpu.VMEM((jt // 128, rows * 2 * F, 128), jnp.float32)],
        ),
        input_output_aliases=aliases,
        compiler_params=pltpu.CompilerParams(
            dimension_semantics=("arbitrary", "arbitrary"), vmem_limit_bytes=52 * 2**20
        ),
        cost_estimate=pl.CostEstimate(
            flops=rows * cols * F * 4 * (2 * NW + LAGS) * 2,
            bytes_accessed=second.size * 2 + rows * cols * LAGS * 2,
            transcendentals=0,
        ),
    )(base, *args)


SCALE = 1.0 / (math.sqrt(NW) * math.sqrt(F))


def on_device(traces, live_flags):
    forward, taper, near, counts, inverse = make_tables()
    white = whiten(traces, live_flags, forward, taper, near, counts)
    per_dev = white.shape[1]
    n_col = lax.axis_size("col")
    me = lax.axis_index("col")
    rows = per_dev * n_col
    second = lax.all_gather(white, "row", axis=1, tiled=True)
    cols = second.shape[1]
    table = jnp.transpose(inverse)
    local_j = jnp.arange(cols, dtype=jnp.int32)
    chan_j = ((local_j // per_dev * n_col + me) * per_dev + local_j % per_dev)[None, :]
    offset = lax.axis_index("row").astype(jnp.int32)[None] * rows
    half = per_dev // 2
    if half % 16 != 0:
        first = lax.all_gather(white, "col", axis=1, tiled=True)
        base = jnp.concatenate([jnp.arange(rows // 8, dtype=jnp.int32), offset])
        return slab([first], second, table, chan_j, base, rows, None)
    ahead, behind = white[:, :half], white[:, half:]
    up = [(s, (s + 1) % n_col) for s in range(n_col)]
    down = [(s, (s - 1) % n_col) for s in range(n_col)]
    groups = jnp.arange(half // 8, dtype=jnp.int32)
    out = None
    for k in range(n_col):
        source_a = (me - k) % n_col
        source_b = (me + k) % n_col
        base = jnp.concatenate(
            [source_a * (per_dev // 8) + groups, (source_b * per_dev + half) // 8 + groups, offset]
        ).astype(jnp.int32)
        parts = [ahead, behind]
        if k < n_col - 1:
            ahead = lax.ppermute(ahead, "col", up)
            behind = lax.ppermute(behind, "col", down)
        out = slab(parts, second, table, chan_j, base, rows, out)
    return out


def solution(mesh):
    in_specs = (P(("row", "col"), None, None), P(("row", "col")))
    out_specs = P("row", "col", None)
    return jax.shard_map(
        on_device, mesh=mesh, in_specs=in_specs, out_specs=out_specs, check_vma=False
    )
```
